256 devices in a mesh: blk: 4 (over x_hi, core), rows: 64 (over z, y, x_lo).
Axes of the slice: x: 4 (x_hi: 2, x_lo: 2; x = x_hi * 2 + x_lo), y: 4, z: 8, core: 2. Of those that a mesh axis runs over, the one named last changes fastest.
Arguments:
- volume: float32 [128, 1024, 1024], P('blk', 'rows'), may hold values from 0 to 1
- col_norm: float32 [128, 1024, 1024], P('blk', 'rows'), may hold values from 0.25 to 2
- measured: float32 [8, 1024, 1024], P(None, 'rows'), may hold values from -6 to 6
- row_norm: float32 [8, 1024, 1024], P(None, 'rows'), may hold values from 0.25 to 2
- tile_table: bfloat16 [64, 128, 128], replicated, may hold values from -0.09375 to 0.09375
- tile_index: int32 [32, 128, 64, 8], P(None, 'blk', 'rows'), may hold values from 0 to 63
- subset: int32 [8], replicated, may hold values from 0 to 31, as said below
- routes: int32 [16384, 1], P(('blk', 'rows')), may hold values from 0 to 63; in each aligned block of 64 rows (0 to 63, 64 to 127, ...) at most 2 rows name the same one
Outputs:
- updated_volume: float32 [128, 1024, 1024], P('blk', 'rows')
The draws below stay inside these ranges and needn't reach their ends.
Inputs may be any that keep to these rules, and one draw needn't show every extreme that they name: `subset`: 8 distinct view numbers of the 32. `routes`: the 64 items of one device (view, then column block) name one detector row tile at most 2 times.
All inputs are finite; a program needn't handle non-finite values.
Results may differ from the reference program's by a relative error of at most 0.0035.
Values may be sent and summed in bfloat16 or wider, within the bound.
No kernel may reach another device: no remote copies, remote signals or barrier semaphores. Data moves between devices by JAX's collectives and lax.ppermute only.
A program may use at most 64 MiB of HBM per device.

```python
import math
import jax
import jax.numpy as jnp
import numpy as np
from jax import lax

C = 1024
COLUMN_SPAN = 128
TILE_ROW_SPAN = 16
DZ = 32
SUBSET_VIEWS = 8
NV = 32
NT = 64
NB = 8
CAP = 2
NR = 1024
NPL = 128
N_BLK = 4
N_ROWS = 64


def draw_subset(key, part):
    key = jax.random.fold_in(key, 11)
    inner_key, order_key = jax.random.split(key)
    middle = jax.random.permutation(inner_key, NV - 2)[:SUBSET_VIEWS - 2].astype(jnp.int32) + 1
    ends = jnp.array([0, NV - 1], dtype=jnp.int32)
    joined = jnp.concatenate([ends, middle])
    order = jax.random.permutation(order_key, SUBSET_VIEWS)
    return joined[order].astype(jnp.int32)


def plant(values, own_key, smallest, high):
    shape = values.shape
    index_at = [jax.random.randint(jax.random.fold_in(own_key, axis), (), 0, shape[axis]) for axis in range(len(shape))]
    values = values.at[tuple(index_at)].set(smallest)
    longest = shape.index(max(shape))
    index_at[longest] = (index_at[longest] + 1) % shape[longest]
    return values.at[tuple(index_at)].set(high)


def levels(stream_key, extent, cuts, low, top_value):
    def one(position, parts):
        heights = jax.random.uniform(jax.random.fold_in(jax.random.fold_in(stream_key, 6), position), (parts,), jnp.float32, low / len(cuts), top_value / len(cuts))
        return jnp.repeat(jnp.exp(heights), extent[position] // parts).reshape((-1,) + (1,) * (len(extent) - position - 1))

    gain = one(*cuts[0])
    for cut in cuts[1:]:
        gain = gain * one(*cut)
    return gain


def assign_block(key, own, number, rows, count, top, bound, slope):
    ranking = jax.random.permutation(key, count)
    packed, ordinary = load_shares(count, rows * top, bound, slope, True), load_shares(count, rows * top, bound, slope, False)
    places = jnp.arange(count)

    def named(tallies, rotation):
        used = int((tallies > 0).sum())
        fixed = max(1, used // 4)
        passed = fixed + (places - fixed + rotation * (used - fixed)) % max(1, count - fixed)
        return jnp.zeros((count,), jnp.int32).at[ranking[jnp.where(places < fixed, places, passed)]].set(jnp.asarray(tallies, jnp.int32))

    tallies = jnp.where(number % 4 == 0, named(packed, number // 4), named(ordinary, number - number // 4 - 1))
    mixed = jax.random.permutation(jax.random.fold_in(own, 3), count)
    source_of, sink = mixed[0:count // 2 * 2:2], mixed[1:count // 2 * 2:2]
    margin = jnp.minimum(tallies[source_of] - 1, bound - tallies[sink]) // 2
    margin = jnp.where((source_of == ranking[0]) | (sink == ranking[0]) | (tallies[sink] == 0), 0, jnp.maximum(margin, 0))
    passed = jax.random.randint(jax.random.fold_in(own, 4), (count // 2,), 0, 1 << 20) % (margin + 1)
    tallies = tallies.at[source_of].add(-passed).at[sink].add(passed)
    labels = jnp.searchsorted(jnp.cumsum(tallies), jnp.arange(rows * top), side="right").astype(jnp.int32)
    listing = labels.reshape(top, rows).T
    listing = listing[jax.random.permutation(jax.random.fold_in(own, 1), rows)]
    rotation = jax.random.randint(jax.random.fold_in(own, 2), (rows, 1), 0, top)
    return jnp.take_along_axis(listing, (jnp.arange(top)[None, :] + rotation) % top, axis=1)


def load_shares(count, total, most, slope, full):
    loads = [(1 << 20) // math.isqrt(grade ** slope) + 1 for grade in range(1, count + 1)]
    largest = most if full else min(most, max(-(-total // count), total * loads[0] // sum(loads)))
    least = 1 if total - largest >= count - 1 else 0
    counts, surplus = [largest] + [least] * (count - 1), total - largest - least * (count - 1)
    while surplus > 0:
        candidates = [i for i in range(1, count) if counts[i] < largest] or [i for i in range(1, count) if counts[i] < most]
        pool, remaining = sum([loads[i] for i in candidates]), surplus
        for i in candidates:
            extra = min(most - counts[i], max(1, remaining * loads[i] // pool), surplus)
            counts[i] = counts[i] + extra
            surplus = surplus - extra
    return np.array(counts)


def normal_values(rng, shape, spread, most, cuts=(), kind=jnp.bfloat16):
    factor_of = levels(rng, shape, cuts, -0.22, 0.18) if cuts else 1.0
    values = jax.random.normal(rng, shape, jnp.float32) * spread * factor_of
    return jnp.minimum(jnp.maximum(values, -most), most).astype(kind)


def setup_inputs(seed: int = 0) -> dict:
    key_of = jax.random.split(jax.random.key(seed), 9)
    volume = jnp.clip(1.0 * jax.random.uniform(key_of[0], (NPL, NR, C), jnp.float32) ** levels(key_of[0], (NPL, NR, C), ((0, 4), (1, 64)), -0.2, 0.2), 0.0, 1.0)
    col_norm = jnp.clip(jnp.exp(math.log(2.0) - 2.0794415 * jax.random.uniform(key_of[1], (NPL, NR, C), jnp.float32) ** levels(key_of[1], (NPL, NR, C), ((0, 4), (1, 64)), -0.2, 0.2)), 0.25, 2.0)
    measured = normal_values(key_of[2], (SUBSET_VIEWS, NR, C), 1.0, 6.0, ((1, 64),), jnp.float32)
    row_norm = jnp.clip(jnp.exp(math.log(2.0) - 2.0794415 * jax.random.uniform(key_of[3], (SUBSET_VIEWS, NR, C), jnp.float32) ** levels(key_of[3], (SUBSET_VIEWS, NR, C), ((1, 64),), -0.2, 0.2)), 0.25, 2.0)
    tile_table = normal_values(key_of[4], (NT, COLUMN_SPAN, COLUMN_SPAN), (DZ * COLUMN_SPAN) ** -0.5, 0.09375)
    tile_index = plant(jax.random.randint(key_of[5], (NV, NPL, N_ROWS, NB), 0, NT), jax.random.fold_in(key_of[5], 1), 0, NT - 1).astype(jnp.int32)
    subset = draw_subset(jax.random.fold_in(key_of[8], 71), 0)
    routes_keys = jax.random.split(jax.random.fold_in(key_of[7], 1), (N_BLK * N_ROWS * SUBSET_VIEWS * NB) // (SUBSET_VIEWS * NB))
    routes_turns = jax.random.permutation(jax.random.fold_in(key_of[7], 3), (N_BLK * N_ROWS * SUBSET_VIEWS * NB) // (SUBSET_VIEWS * NB))
    routes = jax.vmap(lambda own, number: assign_block(jax.random.fold_in(key_of[7], 2), own, number, SUBSET_VIEWS * NB, N_ROWS, 1, CAP, 2))(routes_keys, routes_turns).reshape((N_BLK * N_ROWS * SUBSET_VIEWS * NB, 1))
    return dict(volume=volume, col_norm=col_norm, measured=measured, row_norm=row_norm, tile_table=tile_table, tile_index=tile_index, subset=subset, routes=routes)


def reference(volume, col_norm, measured, row_norm, tile_table, tile_index, subset, routes):
    column_block_count = C // COLUMN_SPAN
    vol_half = volume.astype(jnp.bfloat16).reshape(N_BLK, DZ, N_ROWS, TILE_ROW_SPAN, column_block_count, COLUMN_SPAN)
    dest_rows = routes[:, 0].reshape(N_BLK, N_ROWS, SUBSET_VIEWS, column_block_count)
    targets = jnp.arange(N_ROWS, dtype=jnp.int32)
    chosen = jnp.take(tile_index, subset, axis=0).reshape(SUBSET_VIEWS, N_BLK, DZ, N_ROWS, column_block_count)

    forward_projection = jnp.zeros((SUBSET_VIEWS, N_ROWS, column_block_count, TILE_ROW_SPAN, COLUMN_SPAN), jnp.float32)
    for slab_id in range(N_BLK):
        slab_data = vol_half[slab_id].astype(jnp.float32)

        def forward(inputs):
            index_rows, route_rows = inputs
            weights = tile_table[index_rows].astype(jnp.float32)
            partial_value = jnp.einsum('zdrck,zdcke->dcre', slab_data, weights).astype(jnp.bfloat16)
            hit_table = (route_rows[:, :, None] == targets[None, None, :]).astype(jnp.float32)
            return jnp.einsum('dct,dcre->tcre', hit_table, partial_value.astype(jnp.float32))

        routes_slab = jnp.transpose(dest_rows[slab_id], (1, 0, 2))
        forward_projection = forward_projection + lax.map(forward, (chosen[:, slab_id], routes_slab))

    measurement_blocks = measured.reshape(SUBSET_VIEWS, N_ROWS, TILE_ROW_SPAN, column_block_count, COLUMN_SPAN).transpose(0, 1, 3, 2, 4)
    normalizer_blocks = row_norm.reshape(SUBSET_VIEWS, N_ROWS, TILE_ROW_SPAN, column_block_count, COLUMN_SPAN).transpose(0, 1, 3, 2, 4)
    residual_error = (normalizer_blocks * (measurement_blocks - forward_projection)).astype(jnp.bfloat16)

    pieces = []
    for slab_id in range(N_BLK):
        def backward(running, inputs):
            index_rows, route_rows, res_tile = inputs
            weights = tile_table[index_rows].astype(jnp.float32)
            hit_table = (route_rows[:, :, None] == targets[None, None, :]).astype(jnp.float32)
            tile_blocks = jnp.einsum('dct,tcre->dcre', hit_table, res_tile.astype(jnp.float32))
            return running + jnp.einsum('dcre,zdcke->zdrck', tile_blocks, weights), None

        routes_slab = jnp.transpose(dest_rows[slab_id], (1, 0, 2))
        start = jnp.zeros((DZ, N_ROWS, TILE_ROW_SPAN, column_block_count, COLUMN_SPAN), jnp.float32)
        gathered, _ = lax.scan(backward, start, (chosen[:, slab_id], routes_slab, residual_error))
        pieces.append(gathered)
    gradient = jnp.stack(pieces).reshape(N_BLK * DZ, N_ROWS * TILE_ROW_SPAN, C)
    return jnp.maximum(volume + col_norm * gradient, 0.0)
```

```python
import jax
import jax.numpy as jnp
from jax import lax
from jax.experimental import pallas as pl
from jax.experimental.pallas import tpu as pltpu
from jax.sharding import PartitionSpec as P

HALF = jnp.bfloat16
WIDE = jnp.float32
VMEM = pl.BlockSpec(memory_space=pltpu.VMEM)
SMEM = pl.BlockSpec(memory_space=pltpu.SMEM)


def assign_slots(route_ref, count_ref, slot_ref):
    @pl.loop(0, count_ref.shape[0])
    def _(t):
        count_ref[t] = 0

    @pl.loop(0, slot_ref.shape[0])
    def _(i):
        t = route_ref[i]
        rank = count_ref[t]
        slot_ref[i] = 2 * t + rank
        count_ref[t] = rank + 1


def forward_kernel(
    index_ref, route_ref, volume_ref, table_ref, send_ref, slab, count_ref, slot_ref, number_ref
):
    planes, rows, width = volume_ref.shape
    cols = table_ref.shape[1]
    blocks = width // cols
    views = index_ref.shape[0] // (planes * blocks)
    items = views * blocks
    peers = send_ref.shape[0]
    assign_slots(route_ref, count_ref, slot_ref)

    @pl.loop(0, 2 * peers)
    def _(s):
        number_ref[s] = items

    @pl.loop(0, items)
    def _(i):
        number_ref[slot_ref[i]] = i

    lane = lax.broadcasted_iota(jnp.int32, (8, cols), 1)

    @pl.loop(0, peers)
    def _(t):
        send_ref[t, : 2 * rows, :] = jnp.zeros((2 * rows, cols), HALF)
        numbers = jnp.where(lane == 0, number_ref[2 * t], number_ref[2 * t + 1])
        send_ref[t, 2 * rows :, :] = numbers.astype(WIDE).astype(HALF)

    for c in range(blocks):
        for z in range(planes):
            slab[c, :, z * cols : (z + 1) * cols] = volume_ref[
                z, :, c * cols : (c + 1) * cols
            ].astype(HALF)

    def put(i, value):
        s = slot_ref[i]
        start = pl.multiple_of((s % 2) * rows, rows)
        send_ref[s // 2, pl.ds(start, rows), :] = value.astype(HALF)

    @pl.loop(0, blocks)
    def _(c):
        @pl.loop(0, views // 4)
        def _(quad):
            def tile(v, z):
                return table_ref[index_ref[(v * planes + z) * blocks + c]]

            sums = [jnp.zeros((rows, 2 * cols), WIDE)] * 2
            for z in range(0, planes, 2):
                for h in range(2):
                    v = 4 * quad + 2 * h
                    weights = jnp.concatenate(
                        [
                            jnp.concatenate([tile(v, z), tile(v + 1, z)], axis=1),
                            jnp.concatenate([tile(v, z + 1), tile(v + 1, z + 1)], axis=1),
                        ],
                        axis=0,
                    )
                    sums[h] = sums[h] + jnp.dot(
                        slab[c, :, z * cols : (z + 2) * cols],
                        weights,
                        preferred_element_type=WIDE,
                    )
            for h in range(2):
                v = 4 * quad + 2 * h
                put(v * blocks + c, sums[h][:, :cols])
                put((v + 1) * blocks + c, sums[h][:, cols:])


def collect_kernel(core_ref, number_ref, got_ref, keep_ref, give_ref, total):
    rows = total.shape[1]
    half = keep_ref.shape[0]
    total[...] = jnp.zeros_like(total)

    @pl.loop(0, got_ref.shape[0])
    def _(j):
        for s in range(2):
            i = number_ref[2 * j + s]
            total[i] += got_ref[j, s * rows : (s + 1) * rows, :].astype(WIDE)

    core = core_ref[0]
    keep_ref[...] = total[pl.ds(core * half, half)]
    give_ref[...] = total[pl.ds((1 - core) * half, half)]


def residual_kernel(core_ref, near_ref, far_ref, measured_ref, norm_ref, out_ref):
    half, rows, cols = near_ref.shape
    blocks = measured_ref.shape[2] // cols
    views = half // blocks
    first = core_ref[0] * views
    for v in range(views):
        for c in range(blocks):
            i = v * blocks + c
            at = (first + v, slice(None), slice(c * cols, (c + 1) * cols))
            projection = near_ref[i] + far_ref[i].astype(WIDE)
            out_ref[i] = (norm_ref[at] * (measured_ref[at] - projection)).astype(HALF)


def pack_kernel(core_ref, number_ref, own_ref, other_ref, back_ref, both):
    half, rows, _ = own_ref.shape
    core = core_ref[0]
    both[pl.ds(core * half, half)] = own_ref[...]
    both[pl.ds((1 - core) * half, half)] = other_ref[...]
    both[2 * half] = jnp.zeros(both.shape[1:], HALF)

    @pl.loop(0, back_ref.shape[0])
    def _(j):
        for s in range(2):
            back_ref[j, s * rows : (s + 1) * rows, :] = both[number_ref[2 * j + s]]


def transpose_kernel(table_ref, out_ref):
    @pl.loop(0, table_ref.shape[0])
    def _(t):
        out_ref[t] = table_ref[t].T


def backward_kernel(
    index_ref, route_ref, back_ref, volume_ref, norm_ref, table_ref, out_ref, spread, count_ref, slot_ref
):
    planes, rows, width = volume_ref.shape
    cols = table_ref.shape[1]
    blocks = width // cols
    views = index_ref.shape[0] // (planes * blocks)
    assign_slots(route_ref, count_ref, slot_ref)
    for v in range(views):
        for c in range(blocks):
            s = slot_ref[v * blocks + c]
            start = pl.multiple_of((s % 2) * rows, rows)
            spread[c, :, v * cols : (v + 1) * cols] = back_ref[s // 2, pl.ds(start, rows), :]

    @pl.loop(0, blocks)
    def _(c):
        here = pl.ds(pl.multiple_of(c * cols, cols), cols)

        def tile(v, z):
            return table_ref[index_ref[(v * planes + z) * blocks + c]]

        @pl.loop(0, planes // 4)
        def _(quad):
            for h in range(2):
                z = 4 * quad + 2 * h
                total = jnp.zeros((rows, 2 * cols), WIDE)
                for v in range(0, views, 2):
                    weights = jnp.concatenate(
                        [
                            jnp.concatenate([tile(v, z), tile(v, z + 1)], axis=1),
                            jnp.concatenate([tile(v + 1, z), tile(v + 1, z + 1)], axis=1),
                        ],
                        axis=0,
                    )
                    total = total + jnp.dot(
                        spread[c, :, v * cols : (v + 2) * cols],
                        weights,
                        preferred_element_type=WIDE,
                    )
                for q in range(2):
                    gradient = total[:, q * cols : (q + 1) * cols]
                    out_ref[z + q, :, here] = jnp.maximum(
                        volume_ref[z + q, :, here] + norm_ref[z + q, :, here] * gradient, 0.0
                    )


def local(volume, col_norm, measured, row_norm, tile_table, tile_index, subset, routes):
    planes, rows, width = volume.shape
    views = measured.shape[0]
    cols = tile_table.shape[1]
    blocks = width // cols
    items = views * blocks
    half = items // 2
    peers = lax.axis_size("rows")
    shape = jax.ShapeDtypeStruct
    counters = [pltpu.SMEM((peers,), jnp.int32), pltpu.SMEM((items,), jnp.int32)]

    chosen = jnp.take(tile_index[:, :, 0, :], subset, axis=0).reshape(-1)
    route = routes[:, 0]
    core = (lax.axis_index("blk") % 2).reshape(1)
    turned = pl.pallas_call(
        transpose_kernel,
        out_shape=shape(tile_table.shape, HALF),
        in_specs=[VMEM],
        out_specs=VMEM,
        name="turn_table",
    )(tile_table)

    send = pl.pallas_call(
        forward_kernel,
        out_shape=shape((peers, 2 * rows + 8, cols), HALF),
        in_specs=[SMEM, SMEM, VMEM, VMEM],
        out_specs=VMEM,
        scratch_shapes=[pltpu.VMEM((blocks, rows, planes * cols), HALF)]
        + counters
        + [pltpu.SMEM((2 * peers,), jnp.int32)],
        name="forward",
    )(chosen, route, volume, tile_table)
    got = lax.all_to_all(send, "rows", split_axis=0, concat_axis=0, tiled=True)
    number = got[:, 2 * rows, :2].astype(jnp.int32).reshape(2 * peers)
    keep, give = pl.pallas_call(
        collect_kernel,
        out_shape=[shape((half, rows, cols), WIDE)] * 2,
        in_specs=[SMEM, SMEM, VMEM],
        out_specs=[VMEM, VMEM],
        scratch_shapes=[pltpu.VMEM((items + 1, rows, cols), WIDE)],
        name="collect",
    )(core, number, got)

    swap_core = [(i, i ^ 1) for i in range(4)]
    swap_chip = [(i, i ^ 2) for i in range(4)]
    near = keep + lax.ppermute(give, "blk", swap_core)
    far = lax.ppermute(near.astype(HALF), "blk", swap_chip)
    own = pl.pallas_call(
        residual_kernel,
        out_shape=shape((half, rows, cols), HALF),
        in_specs=[SMEM, VMEM, VMEM, VMEM, VMEM],
        out_specs=VMEM,
        name="residual",
    )(core, near, far, measured, row_norm)
    other = lax.ppermute(own, "blk", swap_core)
    back = pl.pallas_call(
        pack_kernel,
        out_shape=shape((peers, 2 * rows, cols), HALF),
        in_specs=[SMEM, SMEM, VMEM, VMEM],
        out_specs=VMEM,
        scratch_shapes=[pltpu.VMEM((items + 1, rows, cols), HALF)],
        name="pack",
    )(core, number, own, other)
    back = lax.all_to_all(back, "rows", split_axis=0, concat_axis=0, tiled=True)
    return pl.pallas_call(
        backward_kernel,
        out_shape=shape(volume.shape, WIDE),
        in_specs=[SMEM, SMEM, VMEM, VMEM, VMEM, VMEM],
        out_specs=VMEM,
        scratch_shapes=[pltpu.VMEM((blocks, rows, views * cols), HALF)] + counters,
        name="backward",
    )(chosen, route, back, volume, col_norm, turned)


def solution(mesh):
    placed = (
        P("blk", "rows", None),
        P("blk", "rows", None),
        P(None, "rows", None),
        P(None, "rows", None),
        P(),
        P(None, "blk", "rows", None),
        P(),
        P(("blk", "rows"), None),
    )
    return jax.shard_map(
        local, mesh=mesh, in_specs=placed, out_specs=P("blk", "rows", None), check_vma=False
    )
```
